512 devices in a mesh: ma: 64 (over x, z), freq: 8 (over y, core).
Axes of the slice: x: 4, y: 4, z: 16, core: 2. Of those that a mesh axis runs over, the one named last changes fastest.
Arguments:
- visibility: bfloat16 [8, 64, 512, 512], P('freq', 'ma'), may hold values from -6 to 6
- noise_weight: float32 [8, 64, 512], P('freq', 'ma'), may hold values from 0.25 to 2
- transfer: bfloat16 [8, 64, 4, 2, 128, 512], P('freq', 'ma'), may hold values from -0.25 to 0.25
- legendre: bfloat16 [64, 4, 128, 128], P('ma'), may hold values from -0.25 to 0.25
- tile_count: int32 [64], replicated, may hold values from 1 to 4, as said below
Outputs:
- cycle_modes: bfloat16 [128, 64, 512], P('ma', None, 'freq')
The draws below stay inside these ranges and needn't reach their ends.
Inputs may be any that keep to these rules, and one draw needn't show every extreme that they name: Only the first tile_count[j] slots of transfer and legendre for m-mode j are used.
All inputs are finite; a program needn't handle non-finite values.
Results may differ from the reference program's by a relative error of at most 0.019.
Values may be sent and summed in bfloat16 or wider, within the bound.
No kernel may reach another device: no remote copies, remote signals or barrier semaphores. Data moves between devices by JAX's collectives and lax.ppermute only.
A program may use at most 64 MiB of HBM per device.

```python
import math
import jax
import jax.numpy as jnp
from jax import lax

NVIS = 512
LT = 128
SLOTS = 4
NSET = 256
M = 64
FREQ = 8
NRING = 128


def draw_tile_count(key, part):
    key = jax.random.fold_in(key, 7)
    position = jnp.arange(M, dtype=jnp.int32)
    order_rank = jnp.where(position < M // 2, position, 3 * M // 2 - 1 - position)
    stored_full = SLOTS - order_rank * SLOTS // M
    jitter = jax.random.randint(key, (M,), 0, 2, dtype=jnp.int32)
    jitter = jnp.where(position == 0, 0, jitter)
    return jnp.maximum(stored_full - jitter, 1).astype(jnp.int32)


def levels(rng, shape, cuts, least, high):
    def one(dim, shards_of):
        draws = jax.random.uniform(jax.random.fold_in(jax.random.fold_in(rng, 6), dim), (shards_of,), jnp.float32, least / len(cuts), high / len(cuts))
        return jnp.repeat(jnp.exp(draws), shape[dim] // shards_of).reshape((-1,) + (1,) * (len(shape) - dim - 1))

    gain = one(*cuts[0])
    for cut in cuts[1:]:
        gain = gain * one(*cut)
    return gain


def noise(rng, shape, deviation, bound, cuts=(), kind=jnp.bfloat16):
    entries = deviation * jax.random.normal(rng, shape, jnp.float32)
    if cuts:
        entries = entries * levels(rng, shape, cuts, -0.22, 0.18)
    return jnp.clip(entries, -bound, bound).astype(kind)


def setup_inputs(seed: int = 0) -> dict:
    seeds = jax.random.split(jax.random.key(seed), 6)
    visibility = noise(seeds[0], (FREQ, M, NVIS, 2 * NSET), 1.0, 6.0, ((0, 8), (1, 64)))
    noise_weight = jnp.clip(jnp.exp(math.log(2.0) - 2.0794415 * jax.random.uniform(seeds[1], (FREQ, M, NVIS), jnp.float32) ** levels(seeds[1], (FREQ, M, NVIS), ((0, 8), (1, 64)), -0.2, 0.2)), 0.25, 2.0)
    transfer = noise(seeds[2], (FREQ, M, SLOTS, 2, LT, NVIS), NVIS ** -0.5, 0.25, ((0, 8), (1, 64)))
    legendre = noise(seeds[3], (M, SLOTS, NRING, LT), (SLOTS * LT) ** -0.5, 0.25, ((0, 64),))
    tile_count = draw_tile_count(jax.random.fold_in(seeds[5], 71), 0)
    return {"visibility": visibility, "noise_weight": noise_weight, "transfer": transfer, "legendre": legendre, "tile_count": tile_count}


def coeff_tile(beam_tile, weighted):
    real_rows = jnp.dot(beam_tile[0], weighted, preferred_element_type=jnp.float32)
    imag_rows = jnp.dot(beam_tile[1], weighted, preferred_element_type=jnp.float32)
    half_sets = weighted.shape[1] // 2
    real_coeff = real_rows[:, :half_sets] + imag_rows[:, half_sets:]
    imag_coeff = real_rows[:, half_sets:] - imag_rows[:, :half_sets]
    return jnp.concatenate([real_coeff, imag_coeff], axis=1).astype(jnp.bfloat16)


def reference(visibility, noise_weight, transfer, legendre, tile_count):
    def per_column(column):
        cycle_set = legendre[column]
        count = tile_count[column]

        def per_channel(channel, running):
            weighted = (noise_weight[channel, column][:, None] * visibility[channel, column].astype(jnp.float32)).astype(jnp.bfloat16)
            beam_set = transfer[channel, column]

            def add_tile(slot_index, inner):
                coeffs = coeff_tile(beam_set[slot_index], weighted)
                return inner + jnp.dot(cycle_set[slot_index], coeffs, preferred_element_type=jnp.float32)

            return lax.fori_loop(0, count, add_tile, running)

        empty_sum = jnp.zeros((NRING, 2 * NSET), jnp.float32)
        total = lax.fori_loop(0, FREQ, per_channel, empty_sum)
        return (total / FREQ).astype(jnp.bfloat16)

    modes = lax.map(per_column, jnp.arange(M, dtype=jnp.int32))
    return jnp.transpose(modes, (1, 0, 2))
```

```python
import jax
import jax.numpy as jnp
from jax import lax
from jax.experimental import pallas as pl
from jax.experimental.pallas import tpu as pltpu
from jax.sharding import PartitionSpec as P

NVIS = 512
LT = 128
SLOTS = 4
SETS = 512
RINGS = 128
BANDS = 8
CYCLES = 64


def modes_kernel(
    count_ref, vis_hbm, noise_hbm, beam_hbm, cycle_hbm, out_ref,
    vis, noise, beam, cycle, weighted, coeff, acc, sem,
):
    copies = [
        pltpu.make_async_copy(noise_hbm.at[0], noise, sem.at[0]),
        pltpu.make_async_copy(vis_hbm.at[0, 0], vis, sem.at[1]),
    ]
    beam_copies = [
        pltpu.make_async_copy(beam_hbm.at[0, 0, s], beam.at[s], sem.at[2 + s])
        for s in range(SLOTS)
    ]
    cycle_copy = pltpu.make_async_copy(cycle_hbm.at[0], cycle, sem.at[2 + SLOTS])
    for copy in copies + beam_copies + [cycle_copy]:
        copy.start()
    own_count = count_ref[lax.axis_index("ma")]

    copies[0].wait()
    column = jnp.broadcast_to(noise[...], (LT, NVIS)).T
    copies[1].wait()
    for k in range(SETS // 128):
        lanes = pl.ds(128 * k, 128)
        weighted[:, lanes] = (column * vis[:, lanes].astype(jnp.float32)).astype(jnp.bfloat16)

    half = SETS // 2
    for s in range(SLOTS):
        beam_copies[s].wait()
        tile = beam[s].reshape(2 * LT, NVIS)
        rows = jnp.dot(tile, weighted[...], preferred_element_type=jnp.float32)
        real, imag = rows[:LT], rows[LT:]
        keep = s < own_count
        coeff[pl.ds(s * LT, LT), :half] = jnp.where(
            keep, real[:, :half] + imag[:, half:], 0.0
        ).astype(jnp.bfloat16)
        coeff[pl.ds(s * LT, LT), half:] = jnp.where(
            keep, real[:, half:] - imag[:, :half], 0.0
        ).astype(jnp.bfloat16)

    cycle_copy.wait()
    synth = jnp.concatenate([cycle[s] for s in range(SLOTS)], axis=1)
    total = jnp.dot(synth, coeff[...], preferred_element_type=jnp.float32)

    low = lax.broadcasted_iota(jnp.int32, (CYCLES, 128), 1) < 64
    for k in range(SETS // 128):
        acc[k] = total[:, 128 * k : 128 * (k + 1)]
        even = acc[k, pl.ds(0, CYCLES, stride=2), :]
        odd = acc[k, pl.ds(1, CYCLES, stride=2), :]
        out_ref[2 * k] = jnp.where(low, even, pltpu.roll(odd, 64, 1)).astype(jnp.bfloat16)
        out_ref[2 * k + 1] = jnp.where(low, pltpu.roll(even, 64, 1), odd).astype(jnp.bfloat16)


def sum_kernel(band_ref, out_ref):
    total = band_ref[0].astype(jnp.float32)
    for f in range(1, BANDS):
        total += band_ref[f].astype(jnp.float32)
    out_ref[...] = total * (1.0 / BANDS)


def split_kernel(cycle_ref, out_ref):
    rows = cycle_ref[...].astype(jnp.bfloat16)
    out_ref[0] = rows[:, :64]
    out_ref[1] = rows[:, 64:]


def local(visibility, noise_weight, transfer, legendre, tile_count):
    bands = pl.pallas_call(
        modes_kernel,
        out_shape=jax.ShapeDtypeStruct((BANDS, CYCLES, 128), jnp.bfloat16),
        in_specs=[pl.BlockSpec(memory_space=pltpu.SMEM)]
        + [pl.BlockSpec(memory_space=pl.ANY)] * 4,
        out_specs=pl.BlockSpec(memory_space=pltpu.VMEM),
        scratch_shapes=[
            pltpu.VMEM((NVIS, SETS), jnp.bfloat16),
            pltpu.VMEM((1, NVIS), jnp.float32),
            pltpu.VMEM((SLOTS, 2, LT, NVIS), jnp.bfloat16),
            pltpu.VMEM((SLOTS, RINGS, LT), jnp.bfloat16),
            pltpu.VMEM((NVIS, SETS), jnp.bfloat16),
            pltpu.VMEM((SLOTS * LT, SETS), jnp.bfloat16),
            pltpu.VMEM((SETS // 128, RINGS, 128), jnp.float32),
            pltpu.SemaphoreType.DMA((3 + SLOTS,)),
        ],
        compiler_params=pltpu.CompilerParams(vmem_limit_bytes=60 * 1024 * 1024),
    )(tile_count, visibility, noise_weight, transfer, legendre)
    by_band = lax.all_to_all(bands, "freq", 0, 0, tiled=True)
    in_vmem = pl.BlockSpec(memory_space=pltpu.VMEM)
    band_sum = pl.pallas_call(
        sum_kernel,
        out_shape=jax.ShapeDtypeStruct((CYCLES, 128), jnp.float32),
        in_specs=[in_vmem],
        out_specs=in_vmem,
    )(by_band)
    by_cycle = lax.all_to_all(band_sum.reshape(CYCLES, 1, 128), "ma", 0, 0, tiled=True)
    return pl.pallas_call(
        split_kernel,
        out_shape=jax.ShapeDtypeStruct((2, CYCLES, 64), jnp.bfloat16),
        in_specs=[in_vmem],
        out_specs=in_vmem,
    )(by_cycle.reshape(CYCLES, 128))


def solution(mesh):
    return jax.shard_map(
        local,
        mesh=mesh,
        in_specs=(
            P("freq", "ma", None, None),
            P("freq", "ma", None),
            P("freq", "ma", None, None, None, None),
            P("ma", None, None, None),
            P(),
        ),
        out_specs=P("ma", None, "freq"),
        check_vma=False,
    )
```

```python
import jax
import jax.numpy as jnp
from jax import lax
from jax.experimental import pallas as pl
from jax.experimental.pallas import tpu as pltpu
from jax.sharding import PartitionSpec as P

NVIS = 512
LT = 128
SLOTS = 4
SETS = 512
RINGS = 128
BANDS = 8
CYCLES = 64


def modes_kernel(
    count_hbm, vis_hbm, noise_hbm, beam_hbm, cycle_hbm, out_ref,
    vis, noise, beam, cycle, weighted, coeff, acc, count, sem,
):
    copies = [
        pltpu.make_async_copy(noise_hbm.at[0], noise, sem.at[0]),
        pltpu.make_async_copy(vis_hbm.at[0, 0], vis, sem.at[1]),
    ]
    beam_copies = [
        pltpu.make_async_copy(beam_hbm.at[0, 0, s], beam.at[s], sem.at[2 + s])
        for s in range(SLOTS)
    ]
    cycle_copy = pltpu.make_async_copy(cycle_hbm.at[0], cycle, sem.at[2 + SLOTS])
    count_copy = pltpu.make_async_copy(count_hbm, count, sem.at[3 + SLOTS])
    for copy in [count_copy] + copies + beam_copies + [cycle_copy]:
        copy.start()

    copies[0].wait()
    column = jnp.broadcast_to(noise[...], (LT, NVIS)).T
    copies[1].wait()
    for k in range(SETS // 128):
        lanes = pl.ds(128 * k, 128)
        weighted[:, lanes] = (column * vis[:, lanes].astype(jnp.float32)).astype(jnp.bfloat16)

    count_copy.wait()
    own_count = count[lax.axis_index("ma")]
    half = SETS // 2
    for s in range(SLOTS):
        beam_copies[s].wait()
        real = jnp.dot(beam[s, 0], weighted[...], preferred_element_type=jnp.float32)
        imag = jnp.dot(beam[s, 1], weighted[...], preferred_element_type=jnp.float32)
        keep = s < own_count
        coeff[pl.ds(s * LT, LT), :half] = jnp.where(
            keep, real[:, :half] + imag[:, half:], 0.0
        ).astype(jnp.bfloat16)
        coeff[pl.ds(s * LT, LT), half:] = jnp.where(
            keep, real[:, half:] - imag[:, :half], 0.0
        ).astype(jnp.bfloat16)

    cycle_copy.wait()
    synth = jnp.concatenate([cycle[s] for s in range(SLOTS)], axis=1)
    total = jnp.dot(synth, coeff[...], preferred_element_type=jnp.float32)

    low = lax.broadcasted_iota(jnp.int32, (CYCLES, 128), 1) < 64
    for k in range(SETS // 128):
        acc[k] = total[:, 128 * k : 128 * (k + 1)]
        even = acc[k, pl.ds(0, CYCLES, stride=2), :]
        odd = acc[k, pl.ds(1, CYCLES, stride=2), :]
        out_ref[2 * k] = jnp.where(low, even, pltpu.roll(odd, 64, 1)).astype(jnp.bfloat16)
        out_ref[2 * k + 1] = jnp.where(low, pltpu.roll(even, 64, 1), odd).astype(jnp.bfloat16)


def local(visibility, noise_weight, transfer, legendre, tile_count):
    bands = pl.pallas_call(
        modes_kernel,
        out_shape=pltpu.VMEM((BANDS, CYCLES, 128), jnp.bfloat16),
        in_specs=[pl.BlockSpec(memory_space=pl.ANY)] * 5,
        out_specs=pl.BlockSpec(memory_space=pltpu.VMEM),
        scratch_shapes=[
            pltpu.VMEM((NVIS, SETS), jnp.bfloat16),
            pltpu.VMEM((1, NVIS), jnp.float32),
            pltpu.VMEM((SLOTS, 2, LT, NVIS), jnp.bfloat16),
            pltpu.VMEM((SLOTS, RINGS, LT), jnp.bfloat16),
            pltpu.VMEM((NVIS, SETS), jnp.bfloat16),
            pltpu.VMEM((SLOTS * LT, SETS), jnp.bfloat16),
            pltpu.VMEM((SETS // 128, RINGS, 128), jnp.float32),
            pltpu.SMEM((CYCLES,), jnp.int32),
            pltpu.SemaphoreType.DMA((4 + SLOTS,)),
        ],
        compiler_params=pltpu.CompilerParams(vmem_limit_bytes=56 * 1024 * 1024),
    )(tile_count, visibility, noise_weight, transfer, legendre)
    by_band = lax.all_to_all(bands, "freq", 0, 0, tiled=True)
    band_sum = jnp.sum(by_band.astype(jnp.float32), axis=0) * (1.0 / BANDS)
    by_cycle = lax.all_to_all(
        band_sum.reshape(CYCLES, 1, 128), "ma", 0, 0, tiled=True
    ).reshape(CYCLES, 128)
    return jnp.stack([by_cycle[:, :64], by_cycle[:, 64:]]).astype(jnp.bfloat16)


def solution(mesh):
    return jax.shard_map(
        local,
        mesh=mesh,
        in_specs=(
            P("freq", "ma", None, None),
            P("freq", "ma", None),
            P("freq", "ma", None, None, None, None),
            P("ma", None, None, None),
            P(),
        ),
        out_specs=P("ma", None, "freq"),
        check_vma=False,
    )
```

```python
import jax
import jax.numpy as jnp
from jax import lax
from jax.experimental import pallas as pl
from jax.experimental.pallas import tpu as pltpu
from jax.sharding import PartitionSpec as P

NVIS = 512
LT = 128
SLOTS = 4
SETS = 512
RINGS = 128
BANDS = 8
CYCLES = 64

FIRST_BAND = 5
FIRST_MODE = 40
F_ORDER = [(i + FIRST_BAND) % BANDS for i in range(BANDS)]
M_ORDER = [(i + FIRST_MODE) % CYCLES for i in range(CYCLES)]


def modes_kernel(
    count_hbm, vis_hbm, noise_hbm, beam_hbm, cycle_hbm, out_ref,
    vis, noise, beam, cycle, weighted, coeff, acc, count, sem,
):
    copies = [
        pltpu.make_async_copy(noise_hbm.at[0], noise, sem.at[0]),
        pltpu.make_async_copy(vis_hbm.at[0, 0], vis, sem.at[1]),
    ]
    beam_copies = [
        pltpu.make_async_copy(beam_hbm.at[0, 0, s], beam.at[s], sem.at[2 + s])
        for s in range(SLOTS)
    ]
    cycle_copy = pltpu.make_async_copy(cycle_hbm.at[0], cycle, sem.at[2 + SLOTS])
    count_copy = pltpu.make_async_copy(count_hbm, count, sem.at[3 + SLOTS])
    for copy in [count_copy] + copies + beam_copies + [cycle_copy]:
        copy.start()

    copies[0].wait()
    column = jnp.broadcast_to(noise[...], (LT, NVIS)).T
    copies[1].wait()
    for k in range(SETS // 128):
        lanes = pl.ds(128 * k, 128)
        weighted[:, lanes] = (column * vis[:, lanes].astype(jnp.float32)).astype(jnp.bfloat16)

    count_copy.wait()
    own_count = count[lax.axis_index("ma")]
    half = SETS // 2
    for s in range(SLOTS):
        beam_copies[s].wait()
        real = jnp.dot(beam[s, 0], weighted[...], preferred_element_type=jnp.float32)
        imag = jnp.dot(beam[s, 1], weighted[...], preferred_element_type=jnp.float32)
        keep = s < own_count
        coeff[pl.ds(s * LT, LT), :half] = jnp.where(
            keep, real[:, :half] + imag[:, half:], 0.0
        ).astype(jnp.bfloat16)
        coeff[pl.ds(s * LT, LT), half:] = jnp.where(
            keep, real[:, half:] - imag[:, :half], 0.0
        ).astype(jnp.bfloat16)

    cycle_copy.wait()
    synth = jnp.concatenate([cycle[s] for s in range(SLOTS)], axis=1)
    total = jnp.dot(synth, coeff[...], preferred_element_type=jnp.float32)

    low = lax.broadcasted_iota(jnp.int32, (CYCLES, 128), 1) < 64
    for k in range(SETS // 128):
        acc[k] = total[:, 128 * k : 128 * (k + 1)]
        even, odd = (
            jnp.concatenate([
                acc[k, pl.ds(2 * FIRST_MODE + p, CYCLES - FIRST_MODE, stride=2), :],
                acc[k, pl.ds(p, FIRST_MODE, stride=2), :],
            ])
            for p in range(2)
        )
        out_ref[F_ORDER.index(2 * k)] = jnp.where(low, even, pltpu.roll(odd, 64, 1)).astype(jnp.bfloat16)
        out_ref[F_ORDER.index(2 * k + 1)] = jnp.where(low, pltpu.roll(even, 64, 1), odd).astype(jnp.bfloat16)


def local(visibility, noise_weight, transfer, legendre, tile_count):
    bands = pl.pallas_call(
        modes_kernel,
        out_shape=pltpu.VMEM((BANDS, CYCLES, 128), jnp.bfloat16),
        in_specs=[pl.BlockSpec(memory_space=pl.ANY)] * 5,
        out_specs=pl.BlockSpec(memory_space=pltpu.VMEM),
        scratch_shapes=[
            pltpu.VMEM((NVIS, SETS), jnp.bfloat16),
            pltpu.VMEM((1, NVIS), jnp.float32),
            pltpu.VMEM((SLOTS, 2, LT, NVIS), jnp.bfloat16),
            pltpu.VMEM((SLOTS, RINGS, LT), jnp.bfloat16),
            pltpu.VMEM((NVIS, SETS), jnp.bfloat16),
            pltpu.VMEM((SLOTS * LT, SETS), jnp.bfloat16),
            pltpu.VMEM((SETS // 128, RINGS, 128), jnp.float32),
            pltpu.SMEM((CYCLES,), jnp.int32),
            pltpu.SemaphoreType.DMA((4 + SLOTS,)),
        ],
        compiler_params=pltpu.CompilerParams(vmem_limit_bytes=56 * 1024 * 1024),
    )(tile_count, visibility, noise_weight, transfer, legendre)
    by_band = lax.all_to_all(bands, "freq", 0, 0, tiled=True, axis_index_groups=[F_ORDER])
    band_sum = jnp.sum(by_band.astype(jnp.float32), axis=0) * (1.0 / BANDS)
    by_cycle = lax.all_to_all(
        band_sum.reshape(CYCLES, 1, 128), "ma", 0, 0, tiled=True, axis_index_groups=[M_ORDER]
    ).reshape(CYCLES, 128)
    by_cycle = jnp.concatenate([by_cycle[CYCLES - FIRST_MODE :], by_cycle[: CYCLES - FIRST_MODE]])
    return jnp.stack([by_cycle[:, :64], by_cycle[:, 64:]]).astype(jnp.bfloat16)


def solution(mesh):
    return jax.shard_map(
        local,
        mesh=mesh,
        in_specs=(
            P("freq", "ma", None, None),
            P("freq", "ma", None),
            P("freq", "ma", None, None, None, None),
            P("ma", None, None, None),
            P(),
        ),
        out_specs=P("ma", None, "freq"),
        check_vma=False,
    )
```

```python
import jax
import jax.numpy as jnp
from jax import lax
from jax.experimental import pallas as pl
from jax.experimental.pallas import tpu as pltpu
from jax.sharding import PartitionSpec as P

NVIS = 512
LT = 128
SLOTS = 4
SETS = 512
RINGS = 128
BANDS = 8
CYCLES = 64
XS = 4
ZS = 16

FIRST_BAND = 5
FIRST_X = 2
FIRST_Z = 8
F_ORDER = [(i + FIRST_BAND) % BANDS for i in range(BANDS)]
X_ORDER = [(i + FIRST_X) % XS for i in range(XS)]
Z_ORDER = [(i + FIRST_Z) % ZS for i in range(ZS)]
RUNS = [(x * ZS + z, ZS // 2) for x in X_ORDER for z in (FIRST_Z, 0)]
SLAB_GROUPS = [
    [(x * ZS + z) * BANDS + f for x in X_ORDER for f in F_ORDER] for z in range(ZS)
]
LINE_GROUPS = [[x * ZS + z for z in Z_ORDER] for x in range(XS)]


def modes_kernel(
    count_hbm, vis_hbm, noise_hbm, beam_hbm, cycle_hbm, out_ref,
    vis, noise, beam, cycle, weighted, gain, acc, count, sem,
):
    count_copy = pltpu.make_async_copy(count_hbm, count, sem.at[0])
    noise_copy = pltpu.make_async_copy(noise_hbm.at[0], noise, sem.at[1])
    vis_copy = pltpu.make_async_copy(vis_hbm.at[0, 0], vis, sem.at[2])
    cycle_copy = pltpu.make_async_copy(cycle_hbm.at[0], cycle, sem.at[3])
    beam_copy = pltpu.make_async_copy(beam_hbm.at[0, 0], beam, sem.at[4])
    for copy in (count_copy, noise_copy, vis_copy, cycle_copy, beam_copy):
        copy.start()

    noise_copy.wait()
    column = jnp.broadcast_to(noise[...], (LT, NVIS)).T
    vis_copy.wait()
    for k in range(SETS // 128):
        lanes = pl.ds(128 * k, 128)
        weighted[:, lanes] = (column * vis[:, lanes].astype(jnp.float32)).astype(jnp.bfloat16)

    count_copy.wait()
    own_count = count[lax.axis_index("ma")]
    cycle_copy.wait()
    synth = jnp.concatenate(
        [
            jnp.where(s < own_count, cycle[s], jnp.zeros((RINGS, LT), jnp.bfloat16))
            for s in range(SLOTS)
        ],
        axis=1,
    )
    beam_copy.wait()
    for part in range(2):
        tiles = beam[:, part].reshape(SLOTS * LT, NVIS)
        gain[pl.ds(part * RINGS, RINGS)] = jnp.dot(
            synth, tiles, preferred_element_type=jnp.float32
        ).astype(jnp.bfloat16)

    rows = jnp.dot(gain[...], weighted[...], preferred_element_type=jnp.float32)
    real, imag = rows[:RINGS], rows[RINGS:]
    half = SETS // 2
    total = jnp.concatenate(
        [real[:, :half] + imag[:, half:], real[:, half:] - imag[:, :half]], axis=1
    )

    low = lax.broadcasted_iota(jnp.int32, (CYCLES, 128), 1) < 64
    for k in range(SETS // 128):
        acc[k] = total[:, 128 * k : 128 * (k + 1)]
        even, odd = (
            jnp.concatenate([acc[k, pl.ds(2 * d + p, n, stride=2), :] for d, n in RUNS])
            for p in range(2)
        )
        low_band = jnp.where(low, even, pltpu.roll(odd, 64, 1)).astype(jnp.bfloat16)
        high_band = jnp.where(low, pltpu.roll(even, 64, 1), odd).astype(jnp.bfloat16)
        for i in range(XS):
            rows = slice(ZS * i, ZS * (i + 1))
            out_ref[i, F_ORDER.index(2 * k)] = low_band[rows]
            out_ref[i, F_ORDER.index(2 * k + 1)] = high_band[rows]


def local(visibility, noise_weight, transfer, legendre, tile_count):
    bands = pl.pallas_call(
        modes_kernel,
        out_shape=pltpu.VMEM((XS, BANDS, ZS, 128), jnp.bfloat16),
        in_specs=[pl.BlockSpec(memory_space=pl.ANY)] * 5,
        out_specs=pl.BlockSpec(memory_space=pltpu.VMEM),
        scratch_shapes=[
            pltpu.VMEM((NVIS, SETS), jnp.bfloat16),
            pltpu.VMEM((1, NVIS), jnp.float32),
            pltpu.VMEM((SLOTS, 2, LT, NVIS), jnp.bfloat16),
            pltpu.VMEM((SLOTS, RINGS, LT), jnp.bfloat16),
            pltpu.VMEM((NVIS, SETS), jnp.bfloat16),
            pltpu.VMEM((2 * RINGS, NVIS), jnp.bfloat16),
            pltpu.VMEM((SETS // 128, RINGS, 128), jnp.float32),
            pltpu.SMEM((CYCLES,), jnp.int32),
            pltpu.SemaphoreType.DMA((5,)),
        ],
        compiler_params=pltpu.CompilerParams(vmem_limit_bytes=56 * 1024 * 1024),
    )(tile_count, visibility, noise_weight, transfer, legendre)
    by_slab = lax.all_to_all(
        bands.reshape(XS * BANDS, ZS, 128),
        ("ma", "freq"), 0, 0, tiled=True, axis_index_groups=SLAB_GROUPS,
    )
    band_sum = jnp.sum(by_slab.reshape(XS, BANDS, ZS, 128).astype(jnp.float32), axis=1)
    by_line = lax.all_to_all(
        (band_sum * (1.0 / BANDS)).transpose(1, 0, 2),
        "ma", 0, 0, tiled=True, axis_index_groups=LINE_GROUPS,
    )
    modes = by_line.transpose(1, 0, 2)
    modes = jnp.concatenate([modes[:, ZS - FIRST_Z :], modes[:, : ZS - FIRST_Z]], axis=1)
    modes = jnp.concatenate([modes[XS - FIRST_X :], modes[: XS - FIRST_X]]).reshape(CYCLES, 128)
    return jnp.stack([modes[:, :64], modes[:, 64:]]).astype(jnp.bfloat16)


def solution(mesh):
    return jax.shard_map(
        local,
        mesh=mesh,
        in_specs=(
            P("freq", "ma", None, None),
            P("freq", "ma", None),
            P("freq", "ma", None, None, None, None),
            P("ma", None, None, None),
            P(),
        ),
        out_specs=P("ma", None, "freq"),
        check_vma=False,
    )
```

```python
import jax
import jax.numpy as jnp
from jax import lax
from jax.experimental import pallas as pl
from jax.experimental.pallas import tpu as pltpu
from jax.sharding import PartitionSpec as P

NVIS = 512
LT = 128
SLOTS = 4
SETS = 512
RINGS = 128
BANDS = 8
CYCLES = 64
XS = 4
ZS = 16

FIRST_BAND = 5
FIRST_X = 2
FIRST_Z = 8
F_ORDER = [(i + FIRST_BAND) % BANDS for i in range(BANDS)]
X_ORDER = [(i + FIRST_X) % XS for i in range(XS)]
Z_ORDER = [(i + FIRST_Z) % ZS for i in range(ZS)]
RUNS = [(x * ZS + z, ZS // 2) for x in X_ORDER for z in (FIRST_Z, 0)]
SLAB_GROUPS = [
    [(x * ZS + z) * BANDS + f for x in X_ORDER for f in F_ORDER] for z in range(ZS)
]
LINE_GROUPS = [[x * ZS + z for z in Z_ORDER] for x in range(XS)]


def modes_kernel(
    count_hbm, vis_hbm, noise_hbm, beam_hbm, cycle_hbm, out_ref,
    vis, noise, beam, cycle, weighted, gain, acc, count, sem,
):
    count_copy = pltpu.make_async_copy(count_hbm, count, sem.at[0])
    noise_copy = pltpu.make_async_copy(noise_hbm.at[0], noise, sem.at[1])
    vis_copy = pltpu.make_async_copy(vis_hbm.at[0, 0], vis, sem.at[2])
    cycle_copy = pltpu.make_async_copy(cycle_hbm.at[0], cycle, sem.at[3])
    lead_copy, rest_copy = (
        pltpu.make_async_copy(beam_hbm.at[0, 0, pl.ds(s, 2)], beam.at[pl.ds(s, 2)], sem.at[4 + s // 2])
        for s in (0, 2)
    )
    for copy in (count_copy, noise_copy, vis_copy, cycle_copy, lead_copy):
        copy.start()
    count_copy.wait()
    own_count = count[lax.axis_index("ma")]

    @pl.when(own_count > 2)
    def _():
        rest_copy.start()

    @pl.when(own_count <= 2)
    def _():
        beam[pl.ds(2, 2)] = jnp.zeros((2, 2, LT, NVIS), jnp.bfloat16)


    noise_copy.wait()
    column = jnp.broadcast_to(noise[...], (LT, NVIS)).T
    vis_copy.wait()
    for k in range(SETS // 128):
        lanes = pl.ds(128 * k, 128)
        weighted[:, lanes] = (column * vis[:, lanes].astype(jnp.float32)).astype(jnp.bfloat16)

    cycle_copy.wait()
    used = []
    for s in range(SLOTS):
        acc[s] = jnp.where(s < own_count, cycle[s], jnp.zeros((RINGS, LT), jnp.bfloat16)).astype(
            jnp.float32
        )
        rows = [acc[s, pl.ds(2 * d + p, n, stride=2), :] for p in range(2) for d, n in RUNS]
        used.append(jnp.concatenate(rows).astype(jnp.bfloat16))
    synth = jnp.concatenate(used, axis=1)
    lead_copy.wait()

    @pl.when(own_count > 2)
    def _():
        rest_copy.wait()

    for part in range(2):
        tiles = beam[:, part].reshape(SLOTS * LT, NVIS)
        gain[pl.ds(part * RINGS, RINGS)] = jnp.dot(
            synth, tiles, preferred_element_type=jnp.float32
        ).astype(jnp.bfloat16)

    rows = jnp.dot(gain[...], weighted[...], preferred_element_type=jnp.float32)
    real, imag = rows[:RINGS], rows[RINGS:]
    half = SETS // 2
    total = jnp.concatenate(
        [real[:, :half] + imag[:, half:], real[:, half:] - imag[:, :half]], axis=1
    )

    low = lax.broadcasted_iota(jnp.int32, (CYCLES, 128), 1) < 64
    for k in range(SETS // 128):
        lanes = slice(128 * k, 128 * (k + 1))
        even, odd = total[:CYCLES, lanes], total[CYCLES:, lanes]
        low_band = jnp.where(low, even, pltpu.roll(odd, 64, 1)).astype(jnp.bfloat16)
        high_band = jnp.where(low, pltpu.roll(even, 64, 1), odd).astype(jnp.bfloat16)
        for i in range(XS):
            rows = slice(ZS * i, ZS * (i + 1))
            out_ref[i, F_ORDER.index(2 * k)] = low_band[rows]
            out_ref[i, F_ORDER.index(2 * k + 1)] = high_band[rows]


def local(visibility, noise_weight, transfer, legendre, tile_count):
    bands = pl.pallas_call(
        modes_kernel,
        out_shape=pltpu.VMEM((XS, BANDS, ZS, 128), jnp.bfloat16),
        in_specs=[pl.BlockSpec(memory_space=pl.ANY)] * 5,
        out_specs=pl.BlockSpec(memory_space=pltpu.VMEM),
        scratch_shapes=[
            pltpu.VMEM((NVIS, SETS), jnp.bfloat16),
            pltpu.VMEM((1, NVIS), jnp.float32),
            pltpu.VMEM((SLOTS, 2, LT, NVIS), jnp.bfloat16),
            pltpu.VMEM((SLOTS, RINGS, LT), jnp.bfloat16),
            pltpu.VMEM((NVIS, SETS), jnp.bfloat16),
            pltpu.VMEM((2 * RINGS, NVIS), jnp.bfloat16),
            pltpu.VMEM((SLOTS, RINGS, LT), jnp.float32),
            pltpu.SMEM((CYCLES,), jnp.int32),
            pltpu.SemaphoreType.DMA((6,)),
        ],
        compiler_params=pltpu.CompilerParams(vmem_limit_bytes=56 * 1024 * 1024),
    )(tile_count, visibility, noise_weight, transfer, legendre)
    by_slab = lax.all_to_all(
        bands.reshape(XS * BANDS, ZS, 128),
        ("ma", "freq"), 0, 0, tiled=True, axis_index_groups=SLAB_GROUPS,
    )
    band_sum = jnp.sum(by_slab.reshape(XS, BANDS, ZS, 128).astype(jnp.float32), axis=1)
    by_line = lax.all_to_all(
        (band_sum * (1.0 / BANDS)).transpose(1, 0, 2),
        "ma", 0, 0, tiled=True, axis_index_groups=LINE_GROUPS,
    )
    modes = by_line.transpose(1, 0, 2)
    modes = jnp.concatenate([modes[:, ZS - FIRST_Z :], modes[:, : ZS - FIRST_Z]], axis=1)
    modes = jnp.concatenate([modes[XS - FIRST_X :], modes[: XS - FIRST_X]]).reshape(CYCLES, 128)
    return jnp.stack([modes[:, :64], modes[:, 64:]]).astype(jnp.bfloat16)


def solution(mesh):
    return jax.shard_map(
        local,
        mesh=mesh,
        in_specs=(
            P("freq", "ma", None, None),
            P("freq", "ma", None),
            P("freq", "ma", None, None, None, None),
            P("ma", None, None, None),
            P(),
        ),
        out_specs=P("ma", None, "freq"),
        check_vma=False,
    )
```

```python
import jax
import jax.numpy as jnp
from jax import lax
from jax.experimental import pallas as pl
from jax.experimental.pallas import tpu as pltpu
from jax.sharding import PartitionSpec as P

NVIS = 512
LT = 128
SLOTS = 4
SETS = 512
RINGS = 128
BANDS = 8
CYCLES = 64
XS = 4
ZS = 16

FIRST_BAND = 5
FIRST_X = 2
FIRST_Z = 8
F_ORDER = [(i + FIRST_BAND) % BANDS for i in range(BANDS)]
X_ORDER = [(i + FIRST_X) % XS for i in range(XS)]
Z_ORDER = [(i + FIRST_Z) % ZS for i in range(ZS)]
RUNS = [(x * ZS + z, ZS // 2) for x in X_ORDER for z in (FIRST_Z, 0)]
SLAB_GROUPS = [
    [(x * ZS + z) * BANDS + f for x in X_ORDER for f in F_ORDER] for z in range(ZS)
]
LINE_GROUPS = [[x * ZS + z for z in Z_ORDER] for x in range(XS)]


def modes_kernel(
    count_hbm, vis_hbm, noise_hbm, beam_hbm, cycle_hbm, out_ref,
    vis, noise, beam, cycle, weighted, gain, acc, count, sem,
):
    count_copy = pltpu.make_async_copy(count_hbm, count, sem.at[0])
    noise_copy = pltpu.make_async_copy(noise_hbm.at[0], noise, sem.at[1])
    vis_copy = pltpu.make_async_copy(vis_hbm.at[0, 0], vis, sem.at[2])
    cycle_copy = pltpu.make_async_copy(cycle_hbm.at[0], cycle, sem.at[3])
    lead_copy, rest_copy = (
        pltpu.make_async_copy(beam_hbm.at[0, 0, pl.ds(s, 2)], beam.at[pl.ds(s, 2)], sem.at[4 + s // 2])
        for s in (0, 2)
    )
    for copy in (count_copy, noise_copy, vis_copy, cycle_copy, lead_copy):
        copy.start()
    count_copy.wait()
    own_count = count[lax.axis_index("ma")]

    @pl.when(own_count > 2)
    def _():
        rest_copy.start()

    @pl.when(own_count <= 2)
    def _():
        beam[pl.ds(2, 2)] = jnp.zeros((2, 2, LT, NVIS), jnp.bfloat16)


    noise_copy.wait()
    column = jnp.broadcast_to(noise[...], (LT, NVIS)).T
    vis_copy.wait()
    for k in range(SETS // 128):
        lanes = pl.ds(128 * k, 128)
        weighted[:, lanes] = (column * vis[:, lanes].astype(jnp.float32)).astype(jnp.bfloat16)

    cycle_copy.wait()
    used = []
    for s in range(SLOTS):
        acc[s] = jnp.where(s < own_count, cycle[s], jnp.zeros((RINGS, LT), jnp.bfloat16)).astype(
            jnp.float32
        )
        rows = [acc[s, pl.ds(2 * d + p, n, stride=2), :] for p in range(2) for d, n in RUNS]
        used.append((jnp.concatenate(rows) * (1.0 / BANDS)).astype(jnp.bfloat16))
    synth = jnp.concatenate(used, axis=1)
    lead_copy.wait()

    @pl.when(own_count > 2)
    def _():
        rest_copy.wait()

    for part in range(2):
        tiles = beam[:, part].reshape(SLOTS * LT, NVIS)
        gain[pl.ds(part * RINGS, RINGS)] = jnp.dot(
            synth, tiles, preferred_element_type=jnp.float32
        ).astype(jnp.bfloat16)

    rows = jnp.dot(gain[...], weighted[...], preferred_element_type=jnp.float32)
    real, imag = rows[:RINGS], rows[RINGS:]
    half = SETS // 2
    total = jnp.concatenate(
        [real[:, :half] + imag[:, half:], real[:, half:] - imag[:, :half]], axis=1
    )

    low = lax.broadcasted_iota(jnp.int32, (CYCLES, 128), 1) < 64
    for k in range(SETS // 128):
        lanes = slice(128 * k, 128 * (k + 1))
        even, odd = total[:CYCLES, lanes], total[CYCLES:, lanes]
        low_band = jnp.where(low, even, pltpu.roll(odd, 64, 1)).astype(jnp.bfloat16)
        high_band = jnp.where(low, pltpu.roll(even, 64, 1), odd).astype(jnp.bfloat16)
        for i in range(XS):
            rows = slice(ZS * i, ZS * (i + 1))
            out_ref[i, F_ORDER.index(2 * k)] = low_band[rows]
            out_ref[i, F_ORDER.index(2 * k + 1)] = high_band[rows]


def local(visibility, noise_weight, transfer, legendre, tile_count):
    bands = pl.pallas_call(
        modes_kernel,
        out_shape=pltpu.VMEM((XS, BANDS, ZS, 128), jnp.bfloat16),
        in_specs=[pl.BlockSpec(memory_space=pl.ANY)] * 5,
        out_specs=pl.BlockSpec(memory_space=pltpu.VMEM),
        scratch_shapes=[
            pltpu.VMEM((NVIS, SETS), jnp.bfloat16),
            pltpu.VMEM((1, NVIS), jnp.float32),
            pltpu.VMEM((SLOTS, 2, LT, NVIS), jnp.bfloat16),
            pltpu.VMEM((SLOTS, RINGS, LT), jnp.bfloat16),
            pltpu.VMEM((NVIS, SETS), jnp.bfloat16),
            pltpu.VMEM((2 * RINGS, NVIS), jnp.bfloat16),
            pltpu.VMEM((SLOTS, RINGS, LT), jnp.float32),
            pltpu.SMEM((CYCLES,), jnp.int32),
            pltpu.SemaphoreType.DMA((6,)),
        ],
        compiler_params=pltpu.CompilerParams(vmem_limit_bytes=56 * 1024 * 1024),
    )(tile_count, visibility, noise_weight, transfer, legendre)
    by_slab = lax.all_to_all(
        bands.reshape(XS * BANDS, ZS, 128),
        ("ma", "freq"), 0, 0, tiled=True, axis_index_groups=SLAB_GROUPS,
    )
    band_sum = jnp.sum(by_slab.reshape(XS, BANDS, ZS, 128).astype(jnp.float32), axis=1)
    by_line = lax.all_to_all(
        band_sum.transpose(1, 0, 2),
        "ma", 0, 0, tiled=True, axis_index_groups=LINE_GROUPS,
    )
    modes = by_line.reshape(2, ZS // 2, 2, XS // 2, 128).transpose(2, 3, 0, 1, 4)
    modes = lax.rev(modes, (0, 2)).reshape(CYCLES, 128)
    return jnp.stack([modes[:, :64], modes[:, 64:]]).astype(jnp.bfloat16)


def solution(mesh):
    return jax.shard_map(
        local,
        mesh=mesh,
        in_specs=(
            P("freq", "ma", None, None),
            P("freq", "ma", None),
            P("freq", "ma", None, None, None, None),
            P("ma", None, None, None),
            P(),
        ),
        out_specs=P("ma", None, "freq"),
        check_vma=False,
    )
```

```python
import jax
import jax.numpy as jnp
from jax import lax
from jax.experimental import pallas as pl
from jax.experimental.pallas import tpu as pltpu
from jax.sharding import PartitionSpec as P

NVIS = 512
LT = 128
SLOTS = 4
SETS = 512
RINGS = 128
BANDS = 8
CYCLES = 64
XS = 4
ZS = 16

FIRST_BAND = 5
FIRST_X = 2
FIRST_Z = 8
F_ORDER = [(i + FIRST_BAND) % BANDS for i in range(BANDS)]
X_ORDER = [(i + FIRST_X) % XS for i in range(XS)]
Z_ORDER = [(i + FIRST_Z) % ZS for i in range(ZS)]
RUNS = [(x * ZS + z, ZS // 2) for x in X_ORDER for z in (FIRST_Z, 0)]
SLAB_GROUPS = [
    [(x * ZS + z) * BANDS + f for x in X_ORDER for f in F_ORDER] for z in range(ZS)
]
LINE_GROUPS = [[x * ZS + z for z in Z_ORDER] for x in range(XS)]


def modes_kernel(
    count_hbm, vis_hbm, noise_hbm, beam_hbm, cycle_hbm, out_ref,
    vis, noise, beam, cycle, weighted, gain, acc, count, sem,
):
    count_copy = pltpu.make_async_copy(count_hbm, count, sem.at[0])
    noise_copy = pltpu.make_async_copy(noise_hbm.at[0], noise, sem.at[1])
    vis_copy = pltpu.make_async_copy(vis_hbm.at[0, 0], vis, sem.at[2])
    cycle_copy = pltpu.make_async_copy(cycle_hbm.at[0], cycle, sem.at[3])
    lead_copy, rest_copy = (
        pltpu.make_async_copy(beam_hbm.at[0, 0, pl.ds(s, 2)], beam.at[pl.ds(s, 2)], sem.at[4 + s // 2])
        for s in (0, 2)
    )
    for copy in (count_copy, noise_copy, vis_copy, cycle_copy, lead_copy):
        copy.start()
    count_copy.wait()
    own_count = count[lax.axis_index("ma")]

    @pl.when(own_count > 2)
    def _():
        rest_copy.start()

    noise_copy.wait()
    column = jnp.broadcast_to(noise[...], (LT, NVIS)).T
    vis_copy.wait()
    for k in range(SETS // 128):
        lanes = pl.ds(128 * k, 128)
        weighted[:, lanes] = (column * vis[:, lanes].astype(jnp.float32)).astype(jnp.bfloat16)

    cycle_copy.wait()
    used = []
    for s in range(SLOTS):
        acc[s] = jnp.where(s < own_count, cycle[s], jnp.zeros((RINGS, LT), jnp.bfloat16)).astype(
            jnp.float32
        )
        rows = [acc[s, pl.ds(2 * d + p, n, stride=2), :] for p in range(2) for d, n in RUNS]
        used.append((jnp.concatenate(rows) * (1.0 / BANDS)).astype(jnp.bfloat16))
    synth = jnp.concatenate(used, axis=1)
    lead_copy.wait()
    for part in range(2):
        gain[pl.ds(part * RINGS, RINGS)] = jnp.dot(
            synth[:, : 2 * LT], beam[:2, part].reshape(2 * LT, NVIS), preferred_element_type=jnp.float32
        ).astype(jnp.bfloat16)

    @pl.when(own_count > 2)
    def _():
        rest_copy.wait()
        for part in range(2):
            tiles = beam[:, part].reshape(SLOTS * LT, NVIS)
            gain[pl.ds(part * RINGS, RINGS)] = jnp.dot(
                synth, tiles, preferred_element_type=jnp.float32
            ).astype(jnp.bfloat16)

    rows = jnp.dot(gain[...], weighted[...], preferred_element_type=jnp.float32)
    real, imag = rows[:RINGS], rows[RINGS:]
    half = SETS // 2
    total = jnp.concatenate(
        [real[:, :half] + imag[:, half:], real[:, half:] - imag[:, :half]], axis=1
    )

    low = lax.broadcasted_iota(jnp.int32, (CYCLES, 128), 1) < 64
    for k in range(SETS // 128):
        lanes = slice(128 * k, 128 * (k + 1))
        even, odd = total[:CYCLES, lanes], total[CYCLES:, lanes]
        low_band = jnp.where(low, even, pltpu.roll(odd, 64, 1)).astype(jnp.bfloat16)
        high_band = jnp.where(low, pltpu.roll(even, 64, 1), odd).astype(jnp.bfloat16)
        for i in range(XS):
            rows = slice(ZS * i, ZS * (i + 1))
            out_ref[i, F_ORDER.index(2 * k)] = low_band[rows]
            out_ref[i, F_ORDER.index(2 * k + 1)] = high_band[rows]


def local(visibility, noise_weight, transfer, legendre, tile_count):
    bands = pl.pallas_call(
        modes_kernel,
        out_shape=pltpu.VMEM((XS, BANDS, ZS, 128), jnp.bfloat16),
        in_specs=[pl.BlockSpec(memory_space=pl.ANY)] * 5,
        out_specs=pl.BlockSpec(memory_space=pltpu.VMEM),
        scratch_shapes=[
            pltpu.VMEM((NVIS, SETS), jnp.bfloat16),
            pltpu.VMEM((1, NVIS), jnp.float32),
            pltpu.VMEM((SLOTS, 2, LT, NVIS), jnp.bfloat16),
            pltpu.VMEM((SLOTS, RINGS, LT), jnp.bfloat16),
            pltpu.VMEM((NVIS, SETS), jnp.bfloat16),
            pltpu.VMEM((2 * RINGS, NVIS), jnp.bfloat16),
            pltpu.VMEM((SLOTS, RINGS, LT), jnp.float32),
            pltpu.SMEM((CYCLES,), jnp.int32),
            pltpu.SemaphoreType.DMA((6,)),
        ],
        compiler_params=pltpu.CompilerParams(vmem_limit_bytes=56 * 1024 * 1024),
    )(tile_count, visibility, noise_weight, transfer, legendre)
    by_slab = lax.all_to_all(
        bands.reshape(XS * BANDS, ZS, 128),
        ("ma", "freq"), 0, 0, tiled=True, axis_index_groups=SLAB_GROUPS,
    )
    band_sum = jnp.sum(by_slab.reshape(XS, BANDS, ZS, 128).astype(jnp.float32), axis=1)
    by_line = lax.all_to_all(
        band_sum.transpose(1, 0, 2),
        "ma", 0, 0, tiled=True, axis_index_groups=LINE_GROUPS,
    )
    modes = by_line.reshape(2, ZS // 2, 2, XS // 2, 128).transpose(2, 3, 0, 1, 4)
    modes = lax.rev(modes, (0, 2)).reshape(CYCLES, 128)
    return jnp.stack([modes[:, :64], modes[:, 64:]]).astype(jnp.bfloat16)


def solution(mesh):
    return jax.shard_map(
        local,
        mesh=mesh,
        in_specs=(
            P("freq", "ma", None, None),
            P("freq", "ma", None),
            P("freq", "ma", None, None, None, None),
            P("ma", None, None, None),
            P(),
        ),
        out_specs=P("ma", None, "freq"),
        check_vma=False,
    )
```

```python
import jax
import jax.numpy as jnp
from jax import lax
from jax.experimental import pallas as pl
from jax.experimental.pallas import tpu as pltpu
from jax.sharding import PartitionSpec as P

NVIS = 512
LT = 128
SLOTS = 4
SETS = 512
RINGS = 128
BANDS = 8
CYCLES = 64
XS = 4
ZS = 16

FIRST_BAND = 5
FIRST_X = 2
FIRST_Z = 8
F_ORDER = [(i + FIRST_BAND) % BANDS for i in range(BANDS)]
X_ORDER = [(i + FIRST_X) % XS for i in range(XS)]
Z_ORDER = [(i + FIRST_Z) % ZS for i in range(ZS)]
RUNS = [(x * ZS + z, ZS // 2) for x in X_ORDER for z in (FIRST_Z, 0)]
SLAB_GROUPS = [
    [(x * ZS + z) * BANDS + f for x in X_ORDER for f in F_ORDER] for z in range(ZS)
]
LINE_GROUPS = [[x * ZS + z for z in Z_ORDER] for x in range(XS)]


def modes_kernel(
    count_hbm, vis_hbm, noise_hbm, beam_hbm, cycle_hbm, out_ref,
    vis, noise, beam, cycle, weighted, gain, acc, count, sem,
):
    count_copy = pltpu.make_async_copy(count_hbm, count, sem.at[0])
    noise_copy = pltpu.make_async_copy(noise_hbm.at[0], noise, sem.at[1])
    vis_copy = pltpu.make_async_copy(vis_hbm.at[0, 0], vis, sem.at[2])
    cycle_copy = pltpu.make_async_copy(cycle_hbm.at[0], cycle, sem.at[3])
    lead_copy, rest_copy = (
        pltpu.make_async_copy(beam_hbm.at[0, 0, pl.ds(s, 2)], beam.at[pl.ds(s, 2)], sem.at[4 + s // 2])
        for s in (0, 2)
    )
    for copy in (count_copy, noise_copy, cycle_copy, lead_copy, vis_copy):
        copy.start()
    count_copy.wait()
    own_count = count[lax.axis_index("ma")]

    @pl.when(own_count > 2)
    def _():
        rest_copy.start()

    noise_copy.wait()
    column = jnp.broadcast_to(noise[...], (LT, NVIS)).T
    cycle_copy.wait()
    used = []
    for s in range(SLOTS):
        acc[s] = jnp.where(s < own_count, cycle[s], jnp.zeros((RINGS, LT), jnp.bfloat16)).astype(
            jnp.float32
        )
        rows = [acc[s, pl.ds(2 * d + p, n, stride=2), :] for p in range(2) for d, n in RUNS]
        used.append((jnp.concatenate(rows) * (1.0 / BANDS)).astype(jnp.bfloat16))
    synth = jnp.concatenate(used, axis=1)
    lead_copy.wait()
    for part in range(2):
        gain[pl.ds(part * RINGS, RINGS)] = jnp.dot(
            synth[:, : 2 * LT], beam[:2, part].reshape(2 * LT, NVIS), preferred_element_type=jnp.float32
        ).astype(jnp.bfloat16)

    vis_copy.wait()
    for k in range(SETS // 128):
        lanes = pl.ds(128 * k, 128)
        weighted[:, lanes] = (column * vis[:, lanes].astype(jnp.float32)).astype(jnp.bfloat16)

    @pl.when(own_count > 2)
    def _():
        rest_copy.wait()
        for part in range(2):
            tiles = beam[:, part].reshape(SLOTS * LT, NVIS)
            gain[pl.ds(part * RINGS, RINGS)] = jnp.dot(
                synth, tiles, preferred_element_type=jnp.float32
            ).astype(jnp.bfloat16)

    rows = jnp.dot(gain[...], weighted[...], preferred_element_type=jnp.float32)
    real, imag = rows[:RINGS], rows[RINGS:]
    half = SETS // 2
    total = jnp.concatenate(
        [real[:, :half] + imag[:, half:], real[:, half:] - imag[:, :half]], axis=1
    )

    low = lax.broadcasted_iota(jnp.int32, (CYCLES, 128), 1) < 64
    for k in range(SETS // 128):
        lanes = slice(128 * k, 128 * (k + 1))
        even, odd = total[:CYCLES, lanes], total[CYCLES:, lanes]
        low_band = jnp.where(low, even, pltpu.roll(odd, 64, 1)).astype(jnp.bfloat16)
        high_band = jnp.where(low, pltpu.roll(even, 64, 1), odd).astype(jnp.bfloat16)
        for i in range(XS):
            rows = slice(ZS * i, ZS * (i + 1))
            out_ref[i, F_ORDER.index(2 * k)] = low_band[rows]
            out_ref[i, F_ORDER.index(2 * k + 1)] = high_band[rows]


def local(visibility, noise_weight, transfer, legendre, tile_count):
    bands = pl.pallas_call(
        modes_kernel,
        out_shape=pltpu.VMEM((XS, BANDS, ZS, 128), jnp.bfloat16),
        in_specs=[pl.BlockSpec(memory_space=pl.ANY)] * 5,
        out_specs=pl.BlockSpec(memory_space=pltpu.VMEM),
        scratch_shapes=[
            pltpu.VMEM((NVIS, SETS), jnp.bfloat16),
            pltpu.VMEM((1, NVIS), jnp.float32),
            pltpu.VMEM((SLOTS, 2, LT, NVIS), jnp.bfloat16),
            pltpu.VMEM((SLOTS, RINGS, LT), jnp.bfloat16),
            pltpu.VMEM((NVIS, SETS), jnp.bfloat16),
            pltpu.VMEM((2 * RINGS, NVIS), jnp.bfloat16),
            pltpu.VMEM((SLOTS, RINGS, LT), jnp.float32),
            pltpu.SMEM((CYCLES,), jnp.int32),
            pltpu.SemaphoreType.DMA((6,)),
        ],
        compiler_params=pltpu.CompilerParams(vmem_limit_bytes=56 * 1024 * 1024),
    )(tile_count, visibility, noise_weight, transfer, legendre)
    by_slab = lax.all_to_all(
        bands.reshape(XS * BANDS, ZS, 128),
        ("ma", "freq"), 0, 0, tiled=True, axis_index_groups=SLAB_GROUPS,
    )
    band_sum = jnp.sum(by_slab.reshape(XS, BANDS, ZS, 128).astype(jnp.float32), axis=1)
    by_line = lax.all_to_all(
        band_sum.transpose(1, 0, 2),
        "ma", 0, 0, tiled=True, axis_index_groups=LINE_GROUPS,
    )
    modes = by_line.reshape(2, ZS // 2, 2, XS // 2, 128).transpose(2, 3, 0, 1, 4)
    modes = lax.rev(modes, (0, 2)).reshape(CYCLES, 128)
    return jnp.stack([modes[:, :64], modes[:, 64:]]).astype(jnp.bfloat16)


def solution(mesh):
    return jax.shard_map(
        local,
        mesh=mesh,
        in_specs=(
            P("freq", "ma", None, None),
            P("freq", "ma", None),
            P("freq", "ma", None, None, None, None),
            P("ma", None, None, None),
            P(),
        ),
        out_specs=P("ma", None, "freq"),
        check_vma=False,
    )
```
